32 devices in a mesh: ctx: 8 (over y, x, core), tp: 4 (over z).
Axes of the slice: x: 2, y: 2, z: 4, core: 2. Of those that a mesh axis runs over, the one named last changes fastest.
Arguments:
- saved_input: bfloat16 [4096, 4096], P('tp', 'ctx'), may hold values from -8 to 8
- query: bfloat16 [4096, 4096], P('tp', 'ctx'), may hold values from -6 to 6
- key: bfloat16 [4096, 4096], P('tp', 'ctx'), may hold values from -6 to 6
- value: bfloat16 [4096, 4096], P('tp', 'ctx'), may hold values from -6 to 6
- grad_out: bfloat16 [4096, 4096], P('tp', 'ctx'), may hold values from -6 to 6
- filters: bfloat16 [256, 128], P('tp'), may hold values from -0.59765625 to 0.59765625
Outputs:
- grad_query: bfloat16 [4096, 4096], P('tp', 'ctx')
- grad_key: bfloat16 [4096, 4096], P('tp', 'ctx')
- grad_value: bfloat16 [4096, 4096], P('tp', 'ctx')
- grad_filters: float32 [256, 128], P('tp')
- grad_weight: float32 [4096, 4096], P('ctx', 'tp')
The draws below stay inside these ranges and needn't reach their ends.
All inputs are finite; a program needn't handle non-finite values.
Results may differ from the reference program's by a relative error of at most 0.005.
Values may be sent and summed in bfloat16 or wider, within the bound.
No kernel may reach another device: no remote copies, remote signals or barrier semaphores. Data moves between devices by JAX's collectives and lax.ppermute only.
A program may use at most 128 MiB of HBM per device.

```python
import jax
import jax.numpy as jnp
from jax import lax

D_IN = 4096
CH = 4096
GS = 16
FILT = 128
TOKENS = 4096
GROUPS = 256


def raised(array, own_key, source, target, parts, factor):
    owner, partner = [(jnp.arange(array.shape[position]) // (array.shape[position] // parts)).reshape([-1 if axis == position else 1 for axis in range(array.ndim)]) for position in (source, target)]
    chosen = jax.random.permutation(own_key, parts)[partner]
    strong = (owner == chosen) | (owner == (partner + parts // 2) % parts)
    return jnp.where(strong, factor * array, array)


def steps_of(own_key, extent, shards, smallest, largest):
    gain, own = 1.0, jax.random.fold_in(own_key, 6)
    for dim, parts in shards:
        steps = jnp.exp(jax.random.uniform(jax.random.fold_in(own, dim), (parts,), jnp.float32, smallest / len(shards), largest / len(shards)))
        gain = gain * jnp.repeat(steps, extent[dim] // parts).reshape([-1 if axis == dim else 1 for axis in range(len(extent))])
    return gain


def noise(own_key, extent, spread, bound, split=(), kind=jnp.bfloat16):
    factor_of = steps_of(own_key, extent, split, -0.22, 0.18) if split else 1.0
    array = jax.random.normal(own_key, extent, jnp.float32) * spread * factor_of
    return jnp.minimum(jnp.maximum(array, -bound), bound).astype(kind)


def gaussian_with(own_key, extent, scale, limit, shards, heavy, kind=jnp.bfloat16):
    entries = scale * jax.random.normal(own_key, extent, jnp.float32)
    if shards:
        entries = entries * steps_of(own_key, extent, shards, -0.22, 0.18)
    return jnp.clip(raised(entries, jax.random.fold_in(own_key, 3), *heavy), -limit, limit).astype(kind)


def setup_inputs(seed: int = 0) -> dict:
    seeds = jax.random.split(jax.random.key(seed), 7)
    return {
        "saved_input": gaussian_with(seeds[0], (D_IN, TOKENS), 1.0, 8.0, ((0, 4), (1, 8)), (1, 0, 8, 2.0)),
        "query": noise(seeds[1], (CH, TOKENS), 1.0, 6.0, ((0, 4), (1, 8))),
        "key": noise(seeds[2], (CH, TOKENS), 1.0, 6.0, ((0, 4), (1, 8))),
        "value": noise(seeds[3], (CH, TOKENS), 1.0, 6.0, ((0, 4), (1, 8))),
        "grad_out": noise(seeds[4], (CH, TOKENS), 1.0, 6.0, ((0, 4), (1, 8))),
        "filters": noise(seeds[5], (GROUPS, FILT), 0.1, 0.59765625, ((0, 4),)),
    }


def reference(saved_input, query, key, value, grad_out, filters):
    key_value = (key.astype(jnp.float32) * value.astype(jnp.float32)).astype(jnp.bfloat16)
    gate_grad = (query.astype(jnp.float32) * grad_out.astype(jnp.float32)).astype(jnp.bfloat16)
    tap_table = jnp.repeat(filters.astype(jnp.float32), GS, axis=0)
    padded_keys = jnp.concatenate([jnp.zeros((CH, FILT - 1), jnp.bfloat16), key_value], axis=1)
    padded_grads = jnp.concatenate([gate_grad, jnp.zeros((CH, FILT - 1), jnp.bfloat16)], axis=1)

    def forward_step(lag_index, total_sum):
        shifted = lax.dynamic_slice_in_dim(padded_keys, (FILT - 1 - lag_index).astype(jnp.int32), TOKENS, 1)
        column = lax.dynamic_slice_in_dim(tap_table, lag_index.astype(jnp.int32), 1, 1)
        return total_sum + column * shifted.astype(jnp.float32)

    convolved = lax.fori_loop(0, FILT, forward_step, jnp.zeros((CH, TOKENS), jnp.float32))

    def backward_step(lag_index, total_sum):
        shifted = lax.dynamic_slice_in_dim(padded_grads, lag_index.astype(jnp.int32), TOKENS, 1)
        column = lax.dynamic_slice_in_dim(tap_table, lag_index.astype(jnp.int32), 1, 1)
        return total_sum + column * shifted.astype(jnp.float32)

    grad_mixed = lax.fori_loop(0, FILT, backward_step, jnp.zeros((CH, TOKENS), jnp.float32))
    gate_float = gate_grad.astype(jnp.float32)

    def filter_step(carried, lag_index):
        shifted = lax.dynamic_slice_in_dim(padded_keys, (FILT - 1 - lag_index).astype(jnp.int32), TOKENS, 1)
        return carried, jnp.sum(gate_float * shifted.astype(jnp.float32), axis=1)

    unused, columns = lax.scan(filter_step, jnp.zeros((), jnp.float32), jnp.arange(FILT, dtype=jnp.int32))
    grad_filters = columns.reshape(FILT, GROUPS, GS).sum(axis=2).T * (TOKENS * GS) ** -0.5
    grad_query = (grad_out.astype(jnp.float32) * convolved).astype(jnp.bfloat16)
    grad_key = (grad_mixed * value.astype(jnp.float32)).astype(jnp.bfloat16)
    grad_value = (grad_mixed * key.astype(jnp.float32)).astype(jnp.bfloat16)
    grad_weight = lax.dot_general(saved_input, grad_value, (((1,), (1,)), ((), ())), preferred_element_type=jnp.float32) * TOKENS ** -0.5
    return grad_query, grad_key, grad_value, grad_filters, grad_weight
```

```python
import functools
import jax, jax.numpy as jnp
from jax import lax
from jax.experimental import pallas as pl
from jax.experimental.pallas import tpu as pltpu
from jax.sharding import PartitionSpec as P

F32, BF16 = jnp.float32, jnp.bfloat16

def conv_kernel(width, taps, q_ref, k_ref, v_ref, go_ref, kvh_ref, ggh_ref, f_ref, gq_ref, gk_ref, gv_ref, gf_ref, low_ref, high_ref):
    rows, toks = q_ref.shape
    blocks = toks // taps
    for g in range(rows // width):
        r = slice(g * width, (g + 1) * width)
        k = k_ref[r, :].astype(F32)
        v = v_ref[r, :].astype(F32)
        go = go_ref[r, :].astype(F32)
        kv = (k * v).astype(BF16)
        gg = (q_ref[r, :].astype(F32) * go).astype(BF16)
        kvb = [kvh_ref[r, :]] + [kv[:, n * taps:(n + 1) * taps] for n in range(blocks)]
        ggb = [gg[:, n * taps:(n + 1) * taps] for n in range(blocks)] + [ggh_ref[r, :]]
        f = f_ref[g:g + 1, :].astype(F32)
        padded = jnp.concatenate([f, jnp.zeros_like(f)], axis=1)
        band = pltpu.roll(jnp.broadcast_to(padded, (taps, 2 * taps)), 0, 1, stride=1, stride_axis=0).astype(BF16)
        kv_all = jnp.concatenate(kvb, axis=0)
        y = jnp.dot(kv_all, band, preferred_element_type=F32)
        conv = jnp.concatenate(
            [y[(n + 1) * width:(n + 2) * width, :taps] + y[n * width:(n + 1) * width, taps:] for n in range(blocks)], axis=1)
        gq_ref[r, :] = (go * conv).astype(BF16)
        pairs = jnp.concatenate([jnp.concatenate(ggb[:-1], axis=0), jnp.concatenate(ggb[1:], axis=0)], axis=1)
        m = lax.dot_general(pairs, band, (((1,), (1,)), ((), ())), preferred_element_type=F32)
        mixed = jnp.concatenate([m[n * width:(n + 1) * width] for n in range(blocks)], axis=1)
        gk_ref[r, :] = (mixed * v).astype(BF16)
        gv_ref[r, :] = (mixed * k).astype(BF16)
        x = lax.dot_general(kv_all[width:], pairs, (((0,), (0,)), ((), ())), preferred_element_type=F32)
        total = x[:8]
        for a in range(8, taps, 8):
            total = total + pltpu.roll(x[a:a + 8], 2 * taps - a, 1)
        low_ref[8 * g:8 * g + 8, :] = total[:, :taps]
        high_ref[8 * g:8 * g + 8, :] = total[:, taps:]
    lags = rows // width
    total = low_ref[pl.ds(0, lags, stride=8), :]
    for b in range(1, 8):
        both = jnp.concatenate([ref[pl.ds(b, lags, stride=8), :] for ref in (low_ref, high_ref)], axis=1)
        total = total + pltpu.roll(both, 2 * taps - b, 1)[:, :taps]
    gf_ref[...] = total

def conv_call(query, key, value, grad_out, kvh, ggh, filters, step=8):
    channels, toks = key.shape
    groups, taps = filters.shape
    width = channels // groups
    rows = step * width
    wide = pl.BlockSpec((rows, toks), lambda i: (i, 0))
    halo = pl.BlockSpec((rows, taps), lambda i: (i, 0))
    filt = pl.BlockSpec((step, taps), lambda i: (i, 0))
    big = jax.ShapeDtypeStruct((channels, toks), BF16)
    return pl.pallas_call(
        functools.partial(conv_kernel, width, taps),
        grid=(groups // step,),
        in_specs=[wide] * 4 + [halo] * 2 + [filt],
        out_specs=[wide] * 3 + [filt],
        out_shape=[big] * 3 + [jax.ShapeDtypeStruct((groups, taps), F32)],
        scratch_shapes=[pltpu.VMEM((8 * step, taps), F32)] * 2,
        compiler_params=pltpu.CompilerParams(vmem_limit_bytes=48 * 2**20),
        name="conv",
    )(query, key, value, grad_out, kvh, ggh, filters)


def place(relative, bits):
    index = 0
    for bit in bits[1:]:
        index = index * 2 + ((relative >> bit) & 1)
    return ((relative >> bits[0]) & 1) == 1, index


def product_kernel(tp_count, orders, offsets, spot_ref, *refs):
    sources, (own_ref, sibling_ref), outs = refs[: len(offsets)], refs[len(offsets) : len(offsets) + 2], refs[len(offsets) + 2 :]
    side = pl.program_id(0) // (pl.num_programs(0) // 2)
    toks = own_ref.shape[1]
    z, chip = spot_ref[0], spot_ref[1]
    for offset, source in zip(offsets, sources):
        owner = z + offset

        @pl.when((owner >= 0) & (owner < tp_count))
        def _():
            for part in range(source.shape[0]):
                contract = (((1,), (1,)), ((), ()))
                total = lax.dot_general(
                    source[part, :, :toks], own_ref[...], contract, preferred_element_type=F32
                ) + lax.dot_general(
                    source[part, :, toks:], sibling_ref[...], contract, preferred_element_type=F32
                )
                relative = (owner * source.shape[0] + part) ^ chip
                for order, bits in enumerate(orders):
                    goes, index = place(relative, bits)

                    @pl.when((side == order) & goes)
                    def _():
                        outs[2 * order][index] = total.astype(BF16)

                    @pl.when((side == order) & jnp.logical_not(goes))
                    def _():
                        outs[2 * order + 1][index] = total


def product_call(tp_count, orders, offsets, spot, sources, own, sibling):
    channels, toks = own.shape
    parts, rows, _ = sources[0].shape
    tile = min(256, channels // 2)
    steps = channels // tile
    half = tp_count * parts // 2
    whole = pl.BlockSpec(sources[0].shape, lambda i, s: (0, 0, 0))
    tokens = pl.BlockSpec((tile, toks), lambda i, s: (i, 0))
    first = pl.BlockSpec((half, rows, tile), lambda i, s: (0, 0, jnp.minimum(i, steps // 2 - 1)))
    second = pl.BlockSpec((half, rows, tile), lambda i, s: (0, 0, jnp.maximum(i - steps // 2, 0)))
    shape = (half, rows, channels // 2)
    return pl.pallas_call(
        functools.partial(product_kernel, tp_count, orders, offsets),
        grid_spec=pltpu.PrefetchScalarGridSpec(
            num_scalar_prefetch=1,
            grid=(steps,),
            in_specs=[whole] * len(sources) + [tokens] * 2,
            out_specs=[first, first, second, second],
        ),
        out_shape=[jax.ShapeDtypeStruct(shape, kind) for kind in (BF16, F32, BF16, F32)],
        compiler_params=pltpu.CompilerParams(vmem_limit_bytes=40 * 2**20),
        cost_estimate=pl.CostEstimate(
            flops=2 * 2 * half * rows * channels * 2 * toks,
            bytes_accessed=len(sources) * sources[0].size * 2 + own.size * 4 + 2 * half * rows * channels * 3,
            transcendentals=0,
        ),
        name="product",
    )(spot, *sources, own, sibling)


CHUNKS = 4


def along(axis, count, step):
    return lambda value, low, high: lax.ppermute(
        value, axis, [(i, i + step) for i in range(count) if low <= i < high and 0 <= i + step < count]
    )


def shards(saved_input, query, key, value, grad_out, filters):
    channels, toks = key.shape
    groups, taps = filters.shape
    width = channels // groups
    ctx_count, tp_count = lax.axis_size("ctx"), lax.axis_size("tp")
    ctx, z = lax.axis_index("ctx"), lax.axis_index("tp")
    chip, core = ctx // 2, ctx % 2
    chips = ctx_count // 2
    bits = tuple(range(chips.bit_length() - 1))
    orders = (bits, bits[::-1])
    total_tokens = toks * ctx_count

    def flip(array, distance):
        return lax.ppermute(array, "ctx", [(i, i ^ distance) for i in range(ctx_count)])

    parts = chips // tp_count
    rows = saved_input.shape[0] // (2 * parts)
    by_core = saved_input.reshape(parts, 2, rows, toks)
    mine = lax.dynamic_index_in_dim(by_core, core, 1, keepdims=False)
    theirs = lax.dynamic_index_in_dim(by_core, 1 - core, 1, keepdims=False)
    block = jnp.concatenate([mine, flip(theirs, 1)], axis=2)

    def product(a, b):
        return (a.astype(F32) * b.astype(F32)).astype(BF16)

    before = product(key[:, toks - taps :], value[:, toks - taps :])
    after = product(query[:, :taps], grad_out[:, :taps])
    kvh = lax.ppermute(before, "ctx", [(i, i + 1) for i in range(ctx_count - 1)])
    ggh = lax.ppermute(after, "ctx", [(i + 1, i) for i in range(ctx_count - 1)])

    right, left = along("tp", tp_count, 1), along("tp", tp_count, -1)
    size = rows // CHUNKS
    gathered = []
    for c in range(CHUNKS):
        piece = block[:, c * size : (c + 1) * size]
        sources = [(0, piece)]
        up, down = piece, piece
        for s in range(1, tp_count):
            up = right(up, s - 1, tp_count)
            down = left(down, 0, tp_count - s + 1)
            sources += [(-s, up), (s, down)]
        gathered.append(sources)

    grad_query, grad_key, grad_value, lag_sums = conv_call(query, key, value, grad_out, kvh, ggh, filters)
    sibling = flip(grad_value, 1)

    distance = 1
    while distance < ctx_count:
        lag_sums = lag_sums + flip(lag_sums, distance)
        distance *= 2
    grad_filters = lag_sums * (total_tokens * width) ** (-0.5)

    spot = jnp.stack([z, chip]).astype(jnp.int32)
    done = []
    for sources in gathered:
        outs = product_call(
            tp_count, orders, [o for o, _ in sources], spot, [a for _, a in sources], grad_value, sibling
        )
        columns = []
        for order, path in enumerate(orders):
            send, keep = outs[2 * order], outs[2 * order + 1]
            for stage, bit in enumerate(path):
                keep = keep + flip(send, 2 << bit).astype(F32)
                if stage + 1 < len(path):
                    count = keep.shape[0] // 2
                    send, keep = keep[count:].astype(BF16), keep[:count]
            columns.append(keep[0] * total_tokens ** (-0.5))
        done.append(jnp.concatenate(columns, axis=1))
    grad_weight = jnp.concatenate(done, axis=0)
    return (grad_query, grad_key, grad_value, grad_filters, grad_weight)


def solution(mesh):
    placed = (P("tp", "ctx"),) * 5 + (P("tp", None),)
    return jax.shard_map(
        shards,
        mesh=mesh,
        in_specs=placed,
        out_specs=(P("tp", "ctx"),) * 3 + (P("tp", None), P("ctx", "tp")),
        check_vma=False,
    )
```

```python
import functools
import jax, jax.numpy as jnp
from jax import lax
from jax.experimental import pallas as pl
from jax.experimental.pallas import tpu as pltpu
from jax.sharding import PartitionSpec as P

F32, BF16 = jnp.float32, jnp.bfloat16
SHARES, TILE = (12, 11, 9), 512

def conv_kernel(width, taps, q_ref, k_ref, v_ref, go_ref, kvh_ref, ggh_ref, f_ref, after_ref, gq_ref, gk_ref, gv_ref, gf_ref, turned_ref, low_ref, high_ref):
    del after_ref
    rows, toks = q_ref.shape
    blocks = toks // taps
    for g in range(rows // width):
        r = slice(g * width, (g + 1) * width)
        k = k_ref[r, :].astype(F32)
        v = v_ref[r, :].astype(F32)
        go = go_ref[r, :].astype(F32)
        kv = (k * v).astype(BF16)
        gg = (q_ref[r, :].astype(F32) * go).astype(BF16)
        kvb = [kvh_ref[r, :]] + [kv[:, n * taps:(n + 1) * taps] for n in range(blocks)]
        ggb = [gg[:, n * taps:(n + 1) * taps] for n in range(blocks)] + [ggh_ref[r, :]]
        f = f_ref[g:g + 1, :].astype(F32)
        padded = jnp.concatenate([f, jnp.zeros_like(f)], axis=1)
        band = pltpu.roll(jnp.broadcast_to(padded, (taps, 2 * taps)), 0, 1, stride=1, stride_axis=0).astype(BF16)
        kv_all = jnp.concatenate(kvb, axis=0)
        y = jnp.dot(kv_all, band, preferred_element_type=F32)
        conv = jnp.concatenate(
            [y[(n + 1) * width:(n + 2) * width, :taps] + y[n * width:(n + 1) * width, taps:] for n in range(blocks)], axis=1)
        gq_ref[r, :] = (go * conv).astype(BF16)
        pairs = jnp.concatenate([jnp.concatenate(ggb[:-1], axis=0), jnp.concatenate(ggb[1:], axis=0)], axis=1)
        m = lax.dot_general(pairs, band, (((1,), (1,)), ((), ())), preferred_element_type=F32)
        mixed = jnp.concatenate([m[n * width:(n + 1) * width] for n in range(blocks)], axis=1)
        gk_ref[r, :] = (mixed * v).astype(BF16)
        gv_ref[r, :] = (mixed * k).astype(BF16)
        x = lax.dot_general(kv_all[width:], pairs, (((0,), (0,)), ((), ())), preferred_element_type=F32)
        total = x[:8]
        for a in range(8, taps, 8):
            total = total + pltpu.roll(x[a:a + 8], 2 * taps - a, 1)
        low_ref[8 * g:8 * g + 8, :] = total[:, :taps]
        high_ref[8 * g:8 * g + 8, :] = total[:, taps:]
    turned_ref[...] = gv_ref[...].T
    lags = rows // width
    total = low_ref[pl.ds(0, lags, stride=8), :]
    for b in range(1, 8):
        both = jnp.concatenate([ref[pl.ds(b, lags, stride=8), :] for ref in (low_ref, high_ref)], axis=1)
        total = total + pltpu.roll(both, 2 * taps - b, 1)[:, :taps]
    gf_ref[...] = total

def conv_call(query, key, value, grad_out, kvh, ggh, filters, after, step=8):
    channels, toks = key.shape
    groups, taps = filters.shape
    width = channels // groups
    rows = step * width
    wide = pl.BlockSpec((rows, toks), lambda i: (i, 0))
    halo = pl.BlockSpec((rows, taps), lambda i: (i, 0))
    filt = pl.BlockSpec((step, taps), lambda i: (i, 0))
    big = jax.ShapeDtypeStruct((channels, toks), BF16)
    return pl.pallas_call(
        functools.partial(conv_kernel, width, taps),
        grid=(groups // step,),
        in_specs=[wide] * 4 + [halo] * 2 + [filt, pl.BlockSpec(memory_space=pl.ANY)],
        out_specs=[wide] * 3 + [filt, pl.BlockSpec((toks, rows), lambda i: (0, i))],
        out_shape=[big] * 3 + [jax.ShapeDtypeStruct((groups, taps), F32), jax.ShapeDtypeStruct((toks, channels), BF16)],
        scratch_shapes=[pltpu.VMEM((8 * step, taps), F32)] * 2,
        compiler_params=pltpu.CompilerParams(vmem_limit_bytes=48 * 2**20),
        cost_estimate=pl.CostEstimate(
            flops=8 * channels * toks * 2 * taps, bytes_accessed=16 * channels * toks, transcendentals=0
        ),
        name="conv",
    )(query, key, value, grad_out, kvh, ggh, filters, after)


def first_leaves(relative, bits):
    index = 0
    for bit in bits[1:]:
        index = index * 2 + ((relative >> bit) & 1)
    return ((relative >> bits[0]) & 1) == 1, index


def product_kernel(orders, count, spot_ref, *refs):
    sources, (own_ref, sibling_ref), outs, rows_ref = refs[:count], refs[count : count + 2], refs[-1 - 2 * len(orders) : -1], refs[-1]
    blocks, size, _ = rows_ref.shape
    toks = own_ref.shape[0]

    @pl.when(pl.program_id(0) == 0)
    def _():
        entry = 1
        for source in sources:
            for element in range(source.shape[0]):
                owner = spot_ref[entry]
                entry += 1

                @pl.when(owner >= 0)
                def _():
                    for part in range(source.shape[1]):
                        rows_ref[(owner * source.shape[1] + part) ^ spot_ref[0]] = source[element, part]

    rows = rows_ref[...].reshape(blocks * size, 2 * toks)
    total = jnp.dot(rows[:, :toks], own_ref[...], preferred_element_type=F32)
    total = total + jnp.dot(rows[:, toks:], sibling_ref[...], preferred_element_type=F32)
    side = pl.program_id(0) // (pl.num_programs(0) // len(orders))
    for order, bits in enumerate(orders):

        @pl.when(side == order)
        def _():
            for relative in range(blocks):
                goes, index = first_leaves(relative, bits)
                block = total[relative * size : (relative + 1) * size]
                if goes:
                    outs[2 * order][index] = block.astype(BF16)
                else:
                    outs[2 * order + 1][index] = block


def product_call(orders, blocks, spot, sources, own, sibling, after):
    toks, channels = own.shape
    size = sources[0].shape[2]
    tile = min(TILE, channels // 2)
    steps = channels // tile
    run = steps // len(orders)
    half = blocks // 2
    tokens = pl.BlockSpec((toks, tile), lambda i, s: (0, i))
    sides = [
        pl.BlockSpec((half, size, tile), lambda i, s, begin=n * run: (0, 0, jnp.clip(i - begin, 0, run - 1)))
        for n in range(len(orders))
    ]
    shape = (half, size, channels // len(orders))
    return pl.pallas_call(
        functools.partial(product_kernel, orders, len(sources)),
        grid_spec=pltpu.PrefetchScalarGridSpec(
            num_scalar_prefetch=1,
            grid=(steps,),
            in_specs=[pl.BlockSpec(a.shape, lambda i, s: (0, 0, 0, 0)) for a in sources]
            + [tokens] * 2
            + [pl.BlockSpec(memory_space=pl.ANY)] * len(after),
            out_specs=[side for side in sides for _ in range(2)],
            scratch_shapes=[pltpu.VMEM((blocks, size, 2 * toks), BF16)],
        ),
        out_shape=[jax.ShapeDtypeStruct(shape, kind) for kind in (BF16, F32) * len(orders)],
        compiler_params=pltpu.CompilerParams(vmem_limit_bytes=40 * 2**20),
        cost_estimate=pl.CostEstimate(
            flops=4 * blocks * size * channels * toks,
            bytes_accessed=sum(a.size for a in sources) * 2 + own.size * 4 + blocks * size * channels * 3,
            transcendentals=0,
        ),
        name="product",
    )(spot, *sources, own, sibling, *after)


def owners_of(z, count):
    if count == 1:
        return [z]
    group = count // 2
    return owners_of(z, group) + owners_of(facing(z, group), group)


def facing(z, group):
    return jnp.where((z // group) % 2 == 0, (z // group + 1) * group, (z // group) * group - 1)


def hop_pairs(count, group, hop):
    pairs = []
    for base in range(0, count, 2 * group):
        low, high = base + group - 1 - hop, base + group + hop
        pairs += [(low, high), (high, low)] if hop == 0 else [(low + 1, low), (high - 1, high)]
    return pairs


def hop_of(z, group):
    return jnp.where((z // group) % 2 == 0, group - 1 - z % group, z % group)


def gather_groups(piece, axis):
    count, z = lax.axis_size(axis), lax.axis_index(axis)
    stack, owners, group = piece, [z], 1
    while 2 * group < count:
        merged = arrived = lax.ppermute(stack, axis, hop_pairs(count, group, 0))
        for hop in range(1, group):
            arrived = lax.ppermute(arrived, axis, hop_pairs(count, group, hop))
            merged = jnp.where(hop_of(z, group) == hop, arrived, merged)
        stack = [stack, merged] if 4 * group >= count else jnp.concatenate([stack, merged], axis=0)
        owners = owners + owners_of(facing(z, group), group)
        group *= 2
    return stack, owners


def gather_swap(stack, owners, axis):
    count, z = lax.axis_size(axis), lax.axis_index(axis)
    group = count // 2
    arrived = lax.ppermute(stack, axis, hop_pairs(count, group, 0))
    return [stack, arrived], owners + [jnp.where(hop_of(z, group) == 0, owner, -1) for owner in owners_of(facing(z, group), group)]


def gather_rest(arrays, owners, axis, after):
    count, z = lax.axis_size(axis), lax.axis_index(axis)
    group, arrived = count // 2, tied(arrays[-1], after)
    for hop in range(1, group):
        arrived = lax.ppermute(arrived, axis, hop_pairs(count, group, hop))
        arrays = arrays + [arrived]
        owners = owners + [jnp.where(hop_of(z, group) == hop, owner, -1) for owner in owners_of(facing(z, group), group)]
    return arrays, owners


def tied(array, after):
    return lax.optimization_barrier((array, *after))[0] if after else array


def chunk_sizes(rows):
    sizes = [max(16, rows * share // 32 // 16 * 16) for share in SHARES[:-1]]
    return sizes + [rows - sum(sizes)]


def shards(saved_input, query, key, value, grad_out, filters):
    channels, toks = key.shape
    groups, taps = filters.shape
    width = channels // groups
    ctx_count, tp_count = lax.axis_size("ctx"), lax.axis_size("tp")
    ctx = lax.axis_index("ctx")
    chip, core = ctx // 2, ctx % 2
    chips = ctx_count // 2
    bits = tuple(range(chips.bit_length() - 1))
    across = (bits, bits[::-1])
    total_tokens = toks * ctx_count

    def flip(array, distance):
        return lax.ppermute(array, "ctx", [(i, i ^ distance) for i in range(ctx_count)])

    parts = chips // tp_count
    rows = saved_input.shape[0] // (2 * parts)
    by_core = saved_input.reshape(parts, 2, rows, toks)
    mine = lax.dynamic_index_in_dim(by_core, core, 1, keepdims=False)
    theirs = lax.dynamic_index_in_dim(by_core, 1 - core, 1, keepdims=False)
    received = flip(theirs, 1)
    sizes = chunk_sizes(rows)
    parted = []
    for low, high in ((0, sizes[0]), (sizes[0], rows)):
        piece = jnp.concatenate([mine[:, low:high], received[:, low:high]], axis=2)[None]
        halves, owners = gather_groups(piece, "tp")
        parted.append(halves)

    def product(a, b):
        return (a.astype(F32) * b.astype(F32)).astype(BF16)

    before = product(key[:, toks - taps :], value[:, toks - taps :])
    after = product(query[:, :taps], grad_out[:, :taps])
    kvh = lax.ppermute(before, "ctx", [(i, i + 1) for i in range(ctx_count - 1)])
    ggh = lax.ppermute(after, "ctx", [(i + 1, i) for i in range(ctx_count - 1)])

    grad_query, grad_key, grad_value, lag_sums, turned = conv_call(
        query, key, value, grad_out, kvh, ggh, filters, parted[0][1]
    )
    sibling = flip(turned, 1)
    stacks, start = [jnp.concatenate(parted[0], axis=0)], 0
    halves = lax.optimization_barrier((*parted[1], lag_sums))[:2]
    for size in sizes[1:]:
        stacks.append(jnp.concatenate([half[:, :, start : start + size] for half in halves], axis=0))
        start += size

    done, products, sums = [], [], []
    swapped = [gather_swap(stack, owners, "tp") for stack in stacks]
    for number, state in enumerate(swapped):
        arrays, holders = gather_rest(*state, "tp", products[-2:-1] if number else stacks[1:])
        ahead = [arrays[-1] for arrays, _ in swapped[number + 1 : number + 2]]
        orders = across
        spot = jnp.stack([chip] + holders).astype(jnp.int32)
        outs = product_call(orders, chips, spot, arrays, turned, sibling, products[-1:] + ahead)
        products.append(outs[0])
        columns, sums = [], []
        for order, path in enumerate(orders):
            send, keep = outs[2 * order], outs[2 * order + 1]
            for stage, bit in enumerate(path):
                keep = keep + flip(send, 2 << bit).astype(F32)
                if stage + 1 < len(path):
                    count = keep.shape[0] // 2
                    send, keep = keep[count:].astype(BF16), keep[:count]
                    sums.append(send)
            columns.append(keep[0] * total_tokens ** (-0.5))
        done.append(jnp.concatenate(columns, axis=1))
    lag_sums, distance = tied(lag_sums, products[-2:-1]), 1
    while distance < ctx_count:
        lag_sums = lag_sums + flip(lag_sums, distance)
        distance *= 2
    grad_filters = lag_sums * (total_tokens * width) ** (-0.5)
    grad_weight = jnp.concatenate(done, axis=0)
    return (grad_query, grad_key, grad_value, grad_filters, grad_weight)


def solution(mesh):
    placed = (P("tp", "ctx"),) * 5 + (P("tp", None),)
    return jax.shard_map(
        shards,
        mesh=mesh,
        in_specs=placed,
        out_specs=(P("tp", "ctx"),) * 3 + (P("tp", None), P("ctx", "tp")),
        check_vma=False,
    )
```

```python
import functools
import jax, jax.numpy as jnp
from jax import lax
from jax.experimental import pallas as pl
from jax.experimental.pallas import tpu as pltpu
from jax.sharding import PartitionSpec as P

F32, BF16 = jnp.float32, jnp.bfloat16
SHARES, TILE = (12, 11, 9), 512

def conv_kernel(width, taps, q_ref, k_ref, v_ref, go_ref, kvh_ref, ggh_ref, f_ref, after_ref, gq_ref, gk_ref, gv_ref, gf_ref, turned_ref, low_ref, high_ref):
    del after_ref
    rows, toks = q_ref.shape
    blocks = toks // taps
    for g in range(rows // width):
        r = slice(g * width, (g + 1) * width)
        k = k_ref[r, :].astype(F32)
        v = v_ref[r, :].astype(F32)
        go = go_ref[r, :].astype(F32)
        kv = (k * v).astype(BF16)
        gg = (q_ref[r, :].astype(F32) * go).astype(BF16)
        kvb = [kvh_ref[r, :]] + [kv[:, n * taps:(n + 1) * taps] for n in range(blocks)]
        ggb = [gg[:, n * taps:(n + 1) * taps] for n in range(blocks)] + [ggh_ref[r, :]]
        f = f_ref[g:g + 1, :].astype(F32)
        padded = jnp.concatenate([f, jnp.zeros_like(f)], axis=1)
        band = pltpu.roll(jnp.broadcast_to(padded, (taps, 2 * taps)), 0, 1, stride=1, stride_axis=0).astype(BF16)
        kv_all = jnp.concatenate(kvb, axis=0)
        y = jnp.dot(kv_all, band, preferred_element_type=F32)
        conv = jnp.concatenate(
            [y[(n + 1) * width:(n + 2) * width, :taps] + y[n * width:(n + 1) * width, taps:] for n in range(blocks)], axis=1)
        gq_ref[r, :] = (go * conv).astype(BF16)
        pairs = jnp.concatenate([jnp.concatenate(ggb[:-1], axis=0), jnp.concatenate(ggb[1:], axis=0)], axis=1)
        m = lax.dot_general(pairs, band, (((1,), (1,)), ((), ())), preferred_element_type=F32)
        mixed = jnp.concatenate([m[n * width:(n + 1) * width] for n in range(blocks)], axis=1)
        gk_ref[r, :] = (mixed * v).astype(BF16)
        gv_ref[r, :] = (mixed * k).astype(BF16)
        x = lax.dot_general(kv_all[width:], pairs, (((0,), (0,)), ((), ())), preferred_element_type=F32)
        total = x[:8]
        for a in range(8, taps, 8):
            total = total + pltpu.roll(x[a:a + 8], 2 * taps - a, 1)
        low_ref[8 * g:8 * g + 8, :] = total[:, :taps]
        high_ref[8 * g:8 * g + 8, :] = total[:, taps:]
    turned_ref[...] = gv_ref[...].T
    lags = rows // width
    total = low_ref[pl.ds(0, lags, stride=8), :]
    for b in range(1, 8):
        both = jnp.concatenate([ref[pl.ds(b, lags, stride=8), :] for ref in (low_ref, high_ref)], axis=1)
        total = total + pltpu.roll(both, 2 * taps - b, 1)[:, :taps]
    gf_ref[...] = total

def conv_call(query, key, value, grad_out, kvh, ggh, filters, after, step=8):
    channels, toks = key.shape
    groups, taps = filters.shape
    width = channels // groups
    rows = step * width
    wide = pl.BlockSpec((rows, toks), lambda i: (i, 0))
    halo = pl.BlockSpec((rows, taps), lambda i: (i, 0))
    filt = pl.BlockSpec((step, taps), lambda i: (i, 0))
    big = jax.ShapeDtypeStruct((channels, toks), BF16)
    return pl.pallas_call(
        functools.partial(conv_kernel, width, taps),
        grid=(groups // step,),
        in_specs=[wide] * 4 + [halo] * 2 + [filt, pl.BlockSpec(memory_space=pl.ANY)],
        out_specs=[wide] * 3 + [filt, pl.BlockSpec((toks, rows), lambda i: (0, i))],
        out_shape=[big] * 3 + [jax.ShapeDtypeStruct((groups, taps), F32), jax.ShapeDtypeStruct((toks, channels), BF16)],
        scratch_shapes=[pltpu.VMEM((8 * step, taps), F32)] * 2,
        compiler_params=pltpu.CompilerParams(vmem_limit_bytes=48 * 2**20),
        cost_estimate=pl.CostEstimate(
            flops=8 * channels * toks * 2 * taps, bytes_accessed=16 * channels * toks, transcendentals=0
        ),
        name="conv",
    )(query, key, value, grad_out, kvh, ggh, filters, after)


def first_leaves(relative, bits):
    index = 0
    for bit in bits[1:]:
        index = index * 2 + ((relative >> bit) & 1)
    return ((relative >> bits[0]) & 1) == 1, index


def product_kernel(orders, count, spot_ref, *refs):
    sources, (own_ref, sibling_ref), outs, rows_ref = refs[:count], refs[count : count + 2], refs[-1 - 2 * len(orders) : -1], refs[-1]
    blocks, size, _ = rows_ref.shape
    toks = own_ref.shape[0]

    @pl.when(pl.program_id(0) == 0)
    def _():
        entry = 1
        for source in sources:
            for element in range(source.shape[0]):
                owner = spot_ref[entry]
                entry += 1

                @pl.when(owner >= 0)
                def _():
                    for part in range(source.shape[1]):
                        rows_ref[(owner * source.shape[1] + part) ^ spot_ref[0]] = source[element, part]

    rows = rows_ref[...].reshape(blocks * size, 2 * toks)
    total = jnp.dot(rows[:, :toks], own_ref[...], preferred_element_type=F32)
    total = total + jnp.dot(rows[:, toks:], sibling_ref[...], preferred_element_type=F32)
    side = pl.program_id(0) // (pl.num_programs(0) // len(orders))
    for order, bits in enumerate(orders):

        @pl.when(side == order)
        def _():
            for relative in range(blocks):
                goes, index = first_leaves(relative, bits)
                block = total[relative * size : (relative + 1) * size]
                if goes:
                    outs[2 * order][index] = block.astype(BF16)
                else:
                    outs[2 * order + 1][index] = block


def product_call(orders, blocks, spot, sources, own, sibling, after):
    toks, channels = own.shape
    size = sources[0].shape[2]
    tile = min(TILE, channels // 2)
    steps = channels // tile
    run = steps // len(orders)
    half = blocks // 2
    tokens = pl.BlockSpec((toks, tile), lambda i, s: (0, i))
    sides = [
        pl.BlockSpec((half, size, tile), lambda i, s, begin=n * run: (0, 0, jnp.clip(i - begin, 0, run - 1)))
        for n in range(len(orders))
    ]
    shape = (half, size, channels // len(orders))
    return pl.pallas_call(
        functools.partial(product_kernel, orders, len(sources)),
        grid_spec=pltpu.PrefetchScalarGridSpec(
            num_scalar_prefetch=1,
            grid=(steps,),
            in_specs=[pl.BlockSpec(a.shape, lambda i, s: (0, 0, 0, 0)) for a in sources]
            + [tokens] * 2
            + [pl.BlockSpec(memory_space=pl.ANY)] * len(after),
            out_specs=[side for side in sides for _ in range(2)],
            scratch_shapes=[pltpu.VMEM((blocks, size, 2 * toks), BF16)],
        ),
        out_shape=[jax.ShapeDtypeStruct(shape, kind) for kind in (BF16, F32) * len(orders)],
        compiler_params=pltpu.CompilerParams(vmem_limit_bytes=40 * 2**20),
        cost_estimate=pl.CostEstimate(
            flops=4 * blocks * size * channels * toks,
            bytes_accessed=sum(a.size for a in sources) * 2 + own.size * 4 + blocks * size * channels * 3,
            transcendentals=0,
        ),
        name="product",
    )(spot, *sources, own, sibling, *after)


def owners_of(z, count):
    if count == 1:
        return [z]
    group = count // 2
    return owners_of(z, group) + owners_of(facing(z, group), group)


def facing(z, group):
    return jnp.where((z // group) % 2 == 0, (z // group + 1) * group, (z // group) * group - 1)


def hop_pairs(count, group, hop):
    pairs = []
    for base in range(0, count, 2 * group):
        low, high = base + group - 1 - hop, base + group + hop
        pairs += [(low, high), (high, low)] if hop == 0 else [(low + 1, low), (high - 1, high)]
    return pairs


def hop_of(z, group):
    return jnp.where((z // group) % 2 == 0, group - 1 - z % group, z % group)


def gather_groups(piece, axis):
    count, z = lax.axis_size(axis), lax.axis_index(axis)
    stack, owners, group = piece, [z], 1
    while 2 * group < count:
        merged = arrived = lax.ppermute(stack, axis, hop_pairs(count, group, 0))
        for hop in range(1, group):
            arrived = lax.ppermute(arrived, axis, hop_pairs(count, group, hop))
            merged = jnp.where(hop_of(z, group) == hop, arrived, merged)
        stack = [stack, merged] if 4 * group >= count else jnp.concatenate([stack, merged], axis=0)
        owners = owners + owners_of(facing(z, group), group)
        group *= 2
    return stack, owners


def gather_swap(stack, owners, axis):
    count, z = lax.axis_size(axis), lax.axis_index(axis)
    group = count // 2
    arrived = lax.ppermute(stack, axis, hop_pairs(count, group, 0))
    return [stack, arrived], owners + [jnp.where(hop_of(z, group) == 0, owner, -1) for owner in owners_of(facing(z, group), group)]


def gather_rest(arrays, owners, axis, after):
    count, z = lax.axis_size(axis), lax.axis_index(axis)
    group, arrived = count // 2, tied(arrays[-1], after)
    for hop in range(1, group):
        arrived = lax.ppermute(arrived, axis, hop_pairs(count, group, hop))
        arrays = arrays + [arrived]
        owners = owners + [jnp.where(hop_of(z, group) == hop, owner, -1) for owner in owners_of(facing(z, group), group)]
    return arrays, owners


def tied(array, after):
    return lax.optimization_barrier((array, *after))[0] if after else array


def chunk_sizes(rows):
    sizes = [max(16, rows * share // 32 // 16 * 16) for share in SHARES[:-1]]
    return sizes + [rows - sum(sizes)]


def shards(saved_input, query, key, value, grad_out, filters):
    channels, toks = key.shape
    groups, taps = filters.shape
    width = channels // groups
    ctx_count, tp_count = lax.axis_size("ctx"), lax.axis_size("tp")
    ctx = lax.axis_index("ctx")
    chip, core = ctx // 2, ctx % 2
    chips = ctx_count // 2
    bits = tuple(range(chips.bit_length() - 1))
    across = (bits, bits[::-1])
    total_tokens = toks * ctx_count

    def flip(array, distance):
        return lax.ppermute(array, "ctx", [(i, i ^ distance) for i in range(ctx_count)])

    parts = chips // tp_count
    rows = saved_input.shape[0] // (2 * parts)
    by_core = saved_input.reshape(parts, 2, rows, toks)
    mine = lax.dynamic_index_in_dim(by_core, core, 1, keepdims=False)
    theirs = lax.dynamic_index_in_dim(by_core, 1 - core, 1, keepdims=False)
    received = flip(theirs, 1)
    sizes = chunk_sizes(rows)
    parted = []
    for low, high in ((0, sizes[0]), (sizes[0], rows)):
        piece = jnp.concatenate([mine[:, low:high], received[:, low:high]], axis=2)[None]
        halves, owners = gather_groups(piece, "tp")
        parted.append(halves)

    def product(a, b):
        return (a.astype(F32) * b.astype(F32)).astype(BF16)

    before = product(key[:, toks - taps :], value[:, toks - taps :])
    after = product(query[:, :taps], grad_out[:, :taps])
    kvh = lax.ppermute(before, "ctx", [(i, i + 1) for i in range(ctx_count - 1)])
    ggh = lax.ppermute(after, "ctx", [(i + 1, i) for i in range(ctx_count - 1)])

    grad_query, grad_key, grad_value, lag_sums, turned = conv_call(
        query, key, value, grad_out, kvh, ggh, filters, parted[0][1]
    )
    sibling = flip(turned, 1)
    stacks, start = [jnp.concatenate(parted[0], axis=0)], 0
    halves = lax.optimization_barrier((*parted[1], lag_sums))[:2]
    for size in sizes[1:]:
        stacks.append(jnp.concatenate([half[:, :, start : start + size] for half in halves], axis=0))
        start += size

    distance = 1
    while distance < ctx_count:
        lag_sums = lag_sums + flip(lag_sums, distance)
        distance *= 2
    grad_filters = lag_sums * (total_tokens * width) ** (-0.5)

    swapped = [gather_swap(stack, owners, "tp") for stack in stacks]
    products = []
    for number, state in enumerate(swapped):
        arrays, holders = gather_rest(*state, "tp", [lag_sums][: number == 1] if number else stacks[1:])
        ahead = [arrays[-1] for arrays, _ in swapped[number + 1 : number + 2]]
        spot = jnp.stack([chip, *holders]).astype(jnp.int32)
        after = [outs[0] for outs in products[-1:]] + ahead
        products.append(product_call(across, chips, spot, arrays, turned, sibling, after))
    done = []
    for number, outs in enumerate(products):
        late = [outs[0] for outs in products[number + 1 :]] if number + 2 == len(products) else []
        columns = []
        for order, path in enumerate(across):
            send, keep = outs[2 * order], outs[2 * order + 1]
            for stage, bit in enumerate(path):
                keep = keep + flip(send, 2 << bit).astype(F32)
                if stage + 1 < len(path):
                    count = keep.shape[0] // 2
                    send, keep = tied(keep[count:].astype(BF16), late), keep[:count]
            columns.append(keep[0] * total_tokens ** (-0.5))
        done.append(jnp.concatenate(columns, axis=1))
    grad_weight = jnp.concatenate(done, axis=0)
    return (grad_query, grad_key, grad_value, grad_filters, grad_weight)


def solution(mesh):
    placed = (P("tp", "ctx"),) * 5 + (P("tp", None),)
    return jax.shard_map(
        shards,
        mesh=mesh,
        in_specs=placed,
        out_specs=(P("tp", "ctx"),) * 3 + (P("tp", None), P("ctx", "tp")),
        check_vma=False,
    )
```

```python
import functools
import jax, jax.numpy as jnp
from jax import lax
from jax.experimental import pallas as pl
from jax.experimental.pallas import tpu as pltpu
from jax.sharding import PartitionSpec as P

F32, BF16 = jnp.float32, jnp.bfloat16
SHARES, TILE = (12, 12, 8), 512

def conv_kernel(width, taps, q_ref, k_ref, v_ref, go_ref, kvh_ref, ggh_ref, f_ref, after_ref, gq_ref, gk_ref, gv_ref, gf_ref, turned_ref, low_ref, high_ref):
    del after_ref
    rows, toks = q_ref.shape
    blocks = toks // taps
    for g in range(rows // width):
        r = slice(g * width, (g + 1) * width)
        k = k_ref[r, :].astype(F32)
        v = v_ref[r, :].astype(F32)
        go = go_ref[r, :].astype(F32)
        kv = (k * v).astype(BF16)
        gg = (q_ref[r, :].astype(F32) * go).astype(BF16)
        kvb = [kvh_ref[r, :]] + [kv[:, n * taps:(n + 1) * taps] for n in range(blocks)]
        ggb = [gg[:, n * taps:(n + 1) * taps] for n in range(blocks)] + [ggh_ref[r, :]]
        f = f_ref[g:g + 1, :].astype(F32)
        padded = jnp.concatenate([f, jnp.zeros_like(f)], axis=1)
        band = pltpu.roll(jnp.broadcast_to(padded, (taps, 2 * taps)), 0, 1, stride=1, stride_axis=0).astype(BF16)
        kv_all = jnp.concatenate(kvb, axis=0)
        y = jnp.dot(kv_all, band, preferred_element_type=F32)
        conv = jnp.concatenate(
            [y[(n + 1) * width:(n + 2) * width, :taps] + y[n * width:(n + 1) * width, taps:] for n in range(blocks)], axis=1)
        gq_ref[r, :] = (go * conv).astype(BF16)
        pairs = jnp.concatenate([jnp.concatenate(ggb[:-1], axis=0), jnp.concatenate(ggb[1:], axis=0)], axis=1)
        m = lax.dot_general(pairs, band, (((1,), (1,)), ((), ())), preferred_element_type=F32)
        mixed = jnp.concatenate([m[n * width:(n + 1) * width] for n in range(blocks)], axis=1)
        gk_ref[r, :] = (mixed * v).astype(BF16)
        gv_ref[r, :] = (mixed * k).astype(BF16)
        x = lax.dot_general(kv_all[width:], pairs, (((0,), (0,)), ((), ())), preferred_element_type=F32)
        total = x[:8]
        for a in range(8, taps, 8):
            total = total + pltpu.roll(x[a:a + 8], 2 * taps - a, 1)
        low_ref[8 * g:8 * g + 8, :] = total[:, :taps]
        high_ref[8 * g:8 * g + 8, :] = total[:, taps:]
    turned_ref[...] = gv_ref[...].T
    lags = rows // width
    total = low_ref[pl.ds(0, lags, stride=8), :]
    for b in range(1, 8):
        both = jnp.concatenate([ref[pl.ds(b, lags, stride=8), :] for ref in (low_ref, high_ref)], axis=1)
        total = total + pltpu.roll(both, 2 * taps - b, 1)[:, :taps]
    gf_ref[...] = total

def conv_call(query, key, value, grad_out, kvh, ggh, filters, after, step=8):
    channels, toks = key.shape
    groups, taps = filters.shape
    width = channels // groups
    rows = step * width
    wide = pl.BlockSpec((rows, toks), lambda i: (i, 0))
    halo = pl.BlockSpec((rows, taps), lambda i: (i, 0))
    filt = pl.BlockSpec((step, taps), lambda i: (i, 0))
    big = jax.ShapeDtypeStruct((channels, toks), BF16)
    return pl.pallas_call(
        functools.partial(conv_kernel, width, taps),
        grid=(groups // step,),
        in_specs=[wide] * 4 + [halo] * 2 + [filt, pl.BlockSpec(memory_space=pl.ANY)],
        out_specs=[wide] * 3 + [filt, pl.BlockSpec((toks, rows), lambda i: (0, i))],
        out_shape=[big] * 3 + [jax.ShapeDtypeStruct((groups, taps), F32), jax.ShapeDtypeStruct((toks, channels), BF16)],
        scratch_shapes=[pltpu.VMEM((8 * step, taps), F32)] * 2,
        compiler_params=pltpu.CompilerParams(vmem_limit_bytes=48 * 2**20),
        cost_estimate=pl.CostEstimate(
            flops=8 * channels * toks * 2 * taps, bytes_accessed=16 * channels * toks, transcendentals=0
        ),
        name="conv",
    )(query, key, value, grad_out, kvh, ggh, filters, after)


def first_leaves(relative, bits):
    index = 0
    for bit in bits[1:]:
        index = index * 2 + ((relative >> bit) & 1)
    return ((relative >> bits[0]) & 1) == 1, index


def product_kernel(orders, count, spot_ref, *refs):
    sources, (own_ref, sibling_ref), outs, rows_ref = refs[:count], refs[count : count + 2], refs[-1 - 2 * len(orders) : -1], refs[-1]
    blocks, size, _ = rows_ref.shape
    toks = own_ref.shape[0]

    @pl.when(pl.program_id(0) == 0)
    def _():
        entry = 1
        for source in sources:
            for element in range(source.shape[0]):
                owner = spot_ref[entry]
                entry += 1

                @pl.when(owner >= 0)
                def _():
                    for part in range(source.shape[1]):
                        rows_ref[(owner * source.shape[1] + part) ^ spot_ref[0]] = source[element, part]

    rows = rows_ref[...].reshape(blocks * size, 2 * toks)
    total = jnp.dot(rows[:, :toks], own_ref[...], preferred_element_type=F32)
    total = total + jnp.dot(rows[:, toks:], sibling_ref[...], preferred_element_type=F32)
    side = pl.program_id(0) // (pl.num_programs(0) // len(orders))
    for order, bits in enumerate(orders):

        @pl.when(side == order)
        def _():
            for relative in range(blocks):
                goes, index = first_leaves(relative, bits)
                block = total[relative * size : (relative + 1) * size]
                if goes:
                    outs[2 * order][index] = block.astype(BF16)
                else:
                    outs[2 * order + 1][index] = block


def product_call(orders, blocks, spot, sources, own, sibling, after):
    toks, channels = own.shape
    size = sources[0].shape[2]
    tile = min(TILE, channels // 2)
    steps = channels // tile
    run = steps // len(orders)
    half = blocks // 2
    tokens = pl.BlockSpec((toks, tile), lambda i, s: (0, i))
    sides = [
        pl.BlockSpec((half, size, tile), lambda i, s, begin=n * run: (0, 0, jnp.clip(i - begin, 0, run - 1)))
        for n in range(len(orders))
    ]
    shape = (half, size, channels // len(orders))
    return pl.pallas_call(
        functools.partial(product_kernel, orders, len(sources)),
        grid_spec=pltpu.PrefetchScalarGridSpec(
            num_scalar_prefetch=1,
            grid=(steps,),
            in_specs=[pl.BlockSpec(a.shape, lambda i, s: (0, 0, 0, 0)) for a in sources]
            + [tokens] * 2
            + [pl.BlockSpec(memory_space=pl.ANY)] * len(after),
            out_specs=[side for side in sides for _ in range(2)],
            scratch_shapes=[pltpu.VMEM((blocks, size, 2 * toks), BF16)],
        ),
        out_shape=[jax.ShapeDtypeStruct(shape, kind) for kind in (BF16, F32) * len(orders)],
        compiler_params=pltpu.CompilerParams(vmem_limit_bytes=40 * 2**20),
        cost_estimate=pl.CostEstimate(
            flops=4 * blocks * size * channels * toks,
            bytes_accessed=sum(a.size for a in sources) * 2 + own.size * 4 + blocks * size * channels * 3,
            transcendentals=0,
        ),
        name="product",
    )(spot, *sources, own, sibling, *after)


def owners_of(z, count):
    if count == 1:
        return [z]
    group = count // 2
    return owners_of(z, group) + owners_of(facing(z, group), group)


def facing(z, group):
    return jnp.where((z // group) % 2 == 0, (z // group + 1) * group, (z // group) * group - 1)


def hop_pairs(count, group, hop):
    pairs = []
    for base in range(0, count, 2 * group):
        low, high = base + group - 1 - hop, base + group + hop
        pairs += [(low, high), (high, low)] if hop == 0 else [(low + 1, low), (high - 1, high)]
    return pairs


def hop_of(z, group):
    return jnp.where((z // group) % 2 == 0, group - 1 - z % group, z % group)


def gather_groups(piece, axis):
    count, z = lax.axis_size(axis), lax.axis_index(axis)
    stack, owners, group = piece, [z], 1
    while 2 * group < count:
        merged = arrived = lax.ppermute(stack, axis, hop_pairs(count, group, 0))
        for hop in range(1, group):
            arrived = lax.ppermute(arrived, axis, hop_pairs(count, group, hop))
            merged = jnp.where(hop_of(z, group) == hop, arrived, merged)
        stack = [stack, merged] if 4 * group >= count else jnp.concatenate([stack, merged], axis=0)
        owners = owners + owners_of(facing(z, group), group)
        group *= 2
    return stack, owners


def gather_swap(stack, owners, axis):
    count, z = lax.axis_size(axis), lax.axis_index(axis)
    group = count // 2
    arrived = lax.ppermute(stack, axis, hop_pairs(count, group, 0))
    return [stack, arrived], owners + [jnp.where(hop_of(z, group) == 0, owner, -1) for owner in owners_of(facing(z, group), group)]


def gather_rest(arrays, owners, axis, after):
    count, z = lax.axis_size(axis), lax.axis_index(axis)
    group, arrived = count // 2, tied(arrays[-1], after)
    for hop in range(1, group):
        arrived = lax.ppermute(arrived, axis, hop_pairs(count, group, hop))
        arrays = arrays + [arrived]
        owners = owners + [jnp.where(hop_of(z, group) == hop, owner, -1) for owner in owners_of(facing(z, group), group)]
    return arrays, owners


def tied(array, after):
    return lax.optimization_barrier((array, *after))[0] if after else array


def chunk_sizes(rows):
    sizes = [max(16, rows * share // 32 // 16 * 16) for share in SHARES[:-1]]
    return sizes + [rows - sum(sizes)]


def shards(saved_input, query, key, value, grad_out, filters):
    channels, toks = key.shape
    groups, taps = filters.shape
    width = channels // groups
    ctx_count, tp_count = lax.axis_size("ctx"), lax.axis_size("tp")
    ctx = lax.axis_index("ctx")
    chip, core = ctx // 2, ctx % 2
    chips = ctx_count // 2
    bits = tuple(range(chips.bit_length() - 1))
    across = (bits, bits[::-1])
    total_tokens = toks * ctx_count

    def flip(array, distance):
        return lax.ppermute(array, "ctx", [(i, i ^ distance) for i in range(ctx_count)])

    parts = chips // tp_count
    rows = saved_input.shape[0] // (2 * parts)
    by_core = saved_input.reshape(parts, 2, rows, toks)
    mine = lax.dynamic_index_in_dim(by_core, core, 1, keepdims=False)
    theirs = lax.dynamic_index_in_dim(by_core, 1 - core, 1, keepdims=False)
    received = flip(theirs, 1)
    sizes = chunk_sizes(rows)
    parted = []
    for low, high in ((0, sizes[0]), (sizes[0], rows)):
        piece = jnp.concatenate([mine[:, low:high], received[:, low:high]], axis=2)[None]
        halves, owners = gather_groups(piece, "tp")
        parted.append(halves)

    def product(a, b):
        return (a.astype(F32) * b.astype(F32)).astype(BF16)

    before = product(key[:, toks - taps :], value[:, toks - taps :])
    after = product(query[:, :taps], grad_out[:, :taps])
    kvh = lax.ppermute(before, "ctx", [(i, i + 1) for i in range(ctx_count - 1)])
    ggh = lax.ppermute(after, "ctx", [(i + 1, i) for i in range(ctx_count - 1)])

    grad_query, grad_key, grad_value, lag_sums, turned = conv_call(
        query, key, value, grad_out, kvh, ggh, filters, parted[0][1]
    )
    sibling = flip(turned, 1)
    stacks, start = [jnp.concatenate(parted[0], axis=0)], 0
    halves = lax.optimization_barrier((*parted[1], lag_sums))[:2]
    for size in sizes[1:]:
        stacks.append(jnp.concatenate([half[:, :, start : start + size] for half in halves], axis=0))
        start += size

    distance = 1
    while distance < ctx_count:
        lag_sums = lag_sums + flip(lag_sums, distance)
        distance *= 2
    grad_filters = lag_sums * (total_tokens * width) ** (-0.5)

    swapped = [gather_swap(stack, owners, "tp") for stack in stacks]
    products = []
    for number, state in enumerate(swapped):
        arrays, holders = gather_rest(*state, "tp", ([lag_sums], [outs[0] for outs in products[-2:-1]])[number > 1] if number else stacks[1:])
        ahead = [arrays[-1] for arrays, _ in swapped[number + 1 : number + 2]]
        spot = jnp.stack([chip, *holders]).astype(jnp.int32)
        after = [outs[0] for outs in products[-1:]] + ahead
        products.append(product_call(across, chips, spot, arrays, turned, sibling, after))
    done = []
    for number, outs in enumerate(products):
        late = [outs[0] for outs in products[number + 1 :]] if number + 2 == len(products) else []
        columns = []
        for order, path in enumerate(across):
            send, keep = outs[2 * order], outs[2 * order + 1]
            for stage, bit in enumerate(path):
                keep = keep + flip(send, 2 << bit).astype(F32)
                if stage + 1 < len(path):
                    count = keep.shape[0] // 2
                    send, keep = tied(keep[count:].astype(BF16), late), keep[:count]
            columns.append(keep[0] * total_tokens ** (-0.5))
        done.append(jnp.concatenate(columns, axis=1))
    grad_weight = jnp.concatenate(done, axis=0)
    return (grad_query, grad_key, grad_value, grad_filters, grad_weight)


def solution(mesh):
    placed = (P("tp", "ctx"),) * 5 + (P("tp", None),)
    return jax.shard_map(
        shards,
        mesh=mesh,
        in_specs=placed,
        out_specs=(P("tp", "ctx"),) * 3 + (P("tp", None), P("ctx", "tp")),
        check_vma=False,
    )
```

```python
import functools
import jax, jax.numpy as jnp
from jax import lax
from jax.experimental import pallas as pl
from jax.experimental.pallas import tpu as pltpu
from jax.sharding import PartitionSpec as P

F32, BF16 = jnp.float32, jnp.bfloat16
SHARES, TILE = (12, 12, 8), 512

def conv_kernel(width, taps, q_ref, k_ref, v_ref, go_ref, kvh_ref, ggh_ref, f_ref, after_ref, gq_ref, gk_ref, gv_ref, gf_ref, turned_ref, low_ref, high_ref):
    del after_ref
    rows, toks = q_ref.shape
    blocks = toks // taps
    for g in range(rows // width):
        r = slice(g * width, (g + 1) * width)
        k = k_ref[r, :].astype(F32)
        v = v_ref[r, :].astype(F32)
        go = go_ref[r, :].astype(F32)
        kv = (k * v).astype(BF16)
        gg = (q_ref[r, :].astype(F32) * go).astype(BF16)
        kvb = [kvh_ref[r, :]] + [kv[:, n * taps:(n + 1) * taps] for n in range(blocks)]
        ggb = [gg[:, n * taps:(n + 1) * taps] for n in range(blocks)] + [ggh_ref[r, :]]
        f = f_ref[g:g + 1, :].astype(F32)
        padded = jnp.concatenate([f, jnp.zeros_like(f)], axis=1)
        band = pltpu.roll(jnp.broadcast_to(padded, (taps, 2 * taps)), 0, 1, stride=1, stride_axis=0).astype(BF16)
        kv_all = jnp.concatenate(kvb, axis=0)
        y = jnp.dot(kv_all, band, preferred_element_type=F32)
        conv = jnp.concatenate(
            [y[(n + 1) * width:(n + 2) * width, :taps] + y[n * width:(n + 1) * width, taps:] for n in range(blocks)], axis=1)
        gq_ref[r, :] = (go * conv).astype(BF16)
        pairs = jnp.concatenate([jnp.concatenate(ggb[:-1], axis=0), jnp.concatenate(ggb[1:], axis=0)], axis=1)
        m = lax.dot_general(pairs, band, (((1,), (1,)), ((), ())), preferred_element_type=F32)
        mixed = jnp.concatenate([m[n * width:(n + 1) * width] for n in range(blocks)], axis=1)
        gk_ref[r, :] = (mixed * v).astype(BF16)
        gv_ref[r, :] = (mixed * k).astype(BF16)
        x = lax.dot_general(kv_all[width:], pairs, (((0,), (0,)), ((), ())), preferred_element_type=F32)
        total = x[:8]
        for a in range(8, taps, 8):
            total = total + pltpu.roll(x[a:a + 8], 2 * taps - a, 1)
        low_ref[8 * g:8 * g + 8, :] = total[:, :taps]
        high_ref[8 * g:8 * g + 8, :] = total[:, taps:]
    turned_ref[...] = gv_ref[...].T
    lags = rows // width
    total = low_ref[pl.ds(0, lags, stride=8), :]
    for b in range(1, 8):
        both = jnp.concatenate([ref[pl.ds(b, lags, stride=8), :] for ref in (low_ref, high_ref)], axis=1)
        total = total + pltpu.roll(both, 2 * taps - b, 1)[:, :taps]
    gf_ref[...] = total

def conv_call(query, key, value, grad_out, kvh, ggh, filters, after, step=8):
    channels, toks = key.shape
    groups, taps = filters.shape
    width = channels // groups
    rows = step * width
    wide = pl.BlockSpec((rows, toks), lambda i: (i, 0))
    halo = pl.BlockSpec((rows, taps), lambda i: (i, 0))
    filt = pl.BlockSpec((step, taps), lambda i: (i, 0))
    big = jax.ShapeDtypeStruct((channels, toks), BF16)
    return pl.pallas_call(
        functools.partial(conv_kernel, width, taps),
        grid=(groups // step,),
        in_specs=[wide] * 4 + [halo] * 2 + [filt, pl.BlockSpec(memory_space=pl.ANY)],
        out_specs=[wide] * 3 + [filt, pl.BlockSpec((toks, rows), lambda i: (0, i))],
        out_shape=[big] * 3 + [jax.ShapeDtypeStruct((groups, taps), F32), jax.ShapeDtypeStruct((toks, channels), BF16)],
        scratch_shapes=[pltpu.VMEM((8 * step, taps), F32)] * 2,
        compiler_params=pltpu.CompilerParams(vmem_limit_bytes=48 * 2**20),
        cost_estimate=pl.CostEstimate(
            flops=8 * channels * toks * 2 * taps, bytes_accessed=16 * channels * toks, transcendentals=0
        ),
        name="conv",
    )(query, key, value, grad_out, kvh, ggh, filters, after)


def first_leaves(relative, bits):
    index = 0
    for bit in bits[1:]:
        index = index * 2 + ((relative >> bit) & 1)
    return ((relative >> bits[0]) & 1) == 1, index


def product_kernel(orders, count, spot_ref, *refs):
    sources, (own_ref, sibling_ref), outs, rows_ref = refs[:count], refs[count : count + 2], refs[-1 - 2 * len(orders) : -1], refs[-1]
    blocks, size, _ = rows_ref.shape
    toks = own_ref.shape[0]

    @pl.when(pl.program_id(0) == 0)
    def _():
        entry = 1
        for source in sources:
            for element in range(source.shape[0]):
                owner = spot_ref[entry]
                entry += 1

                @pl.when(owner >= 0)
                def _():
                    for part in range(source.shape[1]):
                        rows_ref[(owner * source.shape[1] + part) ^ spot_ref[0]] = source[element, part]

    rows = rows_ref[...].reshape(blocks * size, 2 * toks)
    total = jnp.dot(rows[:, :toks], own_ref[...], preferred_element_type=F32)
    total = total + jnp.dot(rows[:, toks:], sibling_ref[...], preferred_element_type=F32)
    side = pl.program_id(0) // (pl.num_programs(0) // len(orders))
    for order, bits in enumerate(orders):

        @pl.when(side == order)
        def _():
            for relative in range(blocks):
                goes, index = first_leaves(relative, bits)
                block = total[relative * size : (relative + 1) * size]
                if goes:
                    outs[2 * order][index] = block.astype(BF16)
                else:
                    outs[2 * order + 1][index] = block


def product_call(orders, blocks, spot, sources, own, sibling, after):
    toks, channels = own.shape
    size = sources[0].shape[2]
    tile = min(TILE, channels // 2)
    steps = channels // tile
    run = steps // len(orders)
    half = blocks // 2
    tokens = pl.BlockSpec((toks, tile), lambda i, s: (0, i))
    sides = [
        pl.BlockSpec((half, size, tile), lambda i, s, begin=n * run: (0, 0, jnp.clip(i - begin, 0, run - 1)))
        for n in range(len(orders))
    ]
    shape = (half, size, channels // len(orders))
    return pl.pallas_call(
        functools.partial(product_kernel, orders, len(sources)),
        grid_spec=pltpu.PrefetchScalarGridSpec(
            num_scalar_prefetch=1,
            grid=(steps,),
            in_specs=[pl.BlockSpec(a.shape, lambda i, s: (0, 0, 0, 0)) for a in sources]
            + [tokens] * 2
            + [pl.BlockSpec(memory_space=pl.ANY)] * len(after),
            out_specs=[side for side in sides for _ in range(2)],
            scratch_shapes=[pltpu.VMEM((blocks, size, 2 * toks), BF16)],
        ),
        out_shape=[jax.ShapeDtypeStruct(shape, kind) for kind in (BF16, F32) * len(orders)],
        compiler_params=pltpu.CompilerParams(vmem_limit_bytes=40 * 2**20),
        cost_estimate=pl.CostEstimate(
            flops=4 * blocks * size * channels * toks,
            bytes_accessed=sum(a.size for a in sources) * 2 + own.size * 4 + blocks * size * channels * 3,
            transcendentals=0,
        ),
        name="product",
    )(spot, *sources, own, sibling, *after)


def owners_of(z, count):
    if count == 1:
        return [z]
    group = count // 2
    return owners_of(z, group) + owners_of(facing(z, group), group)


def facing(z, group):
    return jnp.where((z // group) % 2 == 0, (z // group + 1) * group, (z // group) * group - 1)


def hop_pairs(count, group, hop):
    pairs = []
    for base in range(0, count, 2 * group):
        low, high = base + group - 1 - hop, base + group + hop
        pairs += [(low, high), (high, low)] if hop == 0 else [(low + 1, low), (high - 1, high)]
    return pairs


def hop_of(z, group):
    return jnp.where((z // group) % 2 == 0, group - 1 - z % group, z % group)


def gather_groups(piece, axis):
    count, z = lax.axis_size(axis), lax.axis_index(axis)
    stack, owners, group = piece, [z], 1
    while 2 * group < count:
        merged = arrived = lax.ppermute(stack, axis, hop_pairs(count, group, 0))
        for hop in range(1, group):
            arrived = lax.ppermute(arrived, axis, hop_pairs(count, group, hop))
            merged = jnp.where(hop_of(z, group) == hop, arrived, merged)
        stack = [stack, merged] if 4 * group >= count else jnp.concatenate([stack, merged], axis=0)
        owners = owners + owners_of(facing(z, group), group)
        group *= 2
    return stack, owners


def gather_swap(stack, owners, axis):
    count, z = lax.axis_size(axis), lax.axis_index(axis)
    group = count // 2
    arrived = lax.ppermute(stack, axis, hop_pairs(count, group, 0))
    return [stack, arrived], owners + [jnp.where(hop_of(z, group) == 0, owner, -1) for owner in owners_of(facing(z, group), group)]


def gather_rest(arrays, owners, axis, after):
    count, z = lax.axis_size(axis), lax.axis_index(axis)
    group, arrived = count // 2, tied(arrays[-1], after)
    for hop in range(1, group):
        arrived = lax.ppermute(arrived, axis, hop_pairs(count, group, hop))
        arrays = arrays + [arrived]
        owners = owners + [jnp.where(hop_of(z, group) == hop, owner, -1) for owner in owners_of(facing(z, group), group)]
    return arrays, owners


def tied(array, after):
    return lax.optimization_barrier((array, *after))[0] if after else array


def chunk_sizes(rows):
    sizes = [max(16, rows * share // 32 // 16 * 16) for share in SHARES[:-1]]
    return sizes + [rows - sum(sizes)]


def shards(saved_input, query, key, value, grad_out, filters):
    channels, toks = key.shape
    groups, taps = filters.shape
    width = channels // groups
    ctx_count, tp_count = lax.axis_size("ctx"), lax.axis_size("tp")
    ctx = lax.axis_index("ctx")
    chip, core = ctx // 2, ctx % 2
    chips = ctx_count // 2
    bits = tuple(range(chips.bit_length() - 1))
    across = (bits, bits[::-1])
    total_tokens = toks * ctx_count

    def flip(array, distance):
        return lax.ppermute(array, "ctx", [(i, i ^ distance) for i in range(ctx_count)])

    parts = chips // tp_count
    rows = saved_input.shape[0] // (2 * parts)
    by_core = saved_input.reshape(parts, 2, rows, toks)
    mine = lax.dynamic_index_in_dim(by_core, core, 1, keepdims=False)
    theirs = lax.dynamic_index_in_dim(by_core, 1 - core, 1, keepdims=False)
    received = flip(theirs, 1)
    sizes = chunk_sizes(rows)
    parted = []
    for low, high in ((0, sizes[0]), (sizes[0], rows)):
        piece = jnp.concatenate([mine[:, low:high], received[:, low:high]], axis=2)[None]
        halves, owners = gather_groups(piece, "tp")
        parted.append(halves)

    def product(a, b):
        return (a.astype(F32) * b.astype(F32)).astype(BF16)

    before = product(key[:, toks - taps :], value[:, toks - taps :])
    after = product(query[:, :taps], grad_out[:, :taps])
    kvh = lax.ppermute(before, "ctx", [(i, i + 1) for i in range(ctx_count - 1)])
    ggh = lax.ppermute(after, "ctx", [(i + 1, i) for i in range(ctx_count - 1)])

    grad_query, grad_key, grad_value, lag_sums, turned = conv_call(
        query, key, value, grad_out, kvh, ggh, filters, parted[0][1]
    )
    sibling = flip(turned, 1)
    stacks, start = [jnp.concatenate(parted[0], axis=0)], 0
    halves = lax.optimization_barrier((*parted[1], lag_sums))[:2]
    for size in sizes[1:]:
        stacks.append(jnp.concatenate([half[:, :, start : start + size] for half in halves], axis=0))
        start += size

    distance = 1
    while distance < ctx_count:
        lag_sums = lag_sums + flip(lag_sums, distance)
        distance *= 2
    grad_filters = lag_sums * (total_tokens * width) ** (-0.5)

    swapped = [gather_swap(stack, owners, "tp") for stack in stacks]
    products = []
    for number, state in enumerate(swapped):
        arrays, holders = gather_rest(*state, "tp", ([lag_sums], [outs[0] for outs in products[-2:-1]])[number > 1] if number else stacks[1:])
        ahead = [arrays[-1] for arrays, _ in swapped[number + 1 : number + 2]]
        spot = jnp.stack([chip, *holders]).astype(jnp.int32)
        after = [outs[0] for outs in products[-1:]] + ahead
        products.append(product_call(across, chips, spot, arrays, turned, sibling, after))
    done, sums = [None] * len(products), []
    for number in reversed(range(len(products))):
        late = [outs[0] for outs in products[number + 1 :]] if number + 2 == len(products) else []
        columns, ended = [], list(sums)
        for order, path in enumerate(across):
            send, keep = products[number][2 * order : 2 * order + 2]
            for stage, bit in enumerate(path):
                arrived = flip(send, 2 << bit)
                if stage + 1 < len(path):
                    keep = keep + arrived.astype(F32)
                    count = keep.shape[0] // 2
                    send, keep = tied(keep[count:].astype(BF16), late), keep[:count]
                    sums += [send] if number + 1 == len(products) else []
                else:
                    keep = keep + tied(arrived, ended).astype(F32)
            columns.append(keep[0] * total_tokens ** (-0.5))
        done[number] = jnp.concatenate(columns, axis=1)
    grad_weight = jnp.concatenate(done, axis=0)
    return (grad_query, grad_key, grad_value, grad_filters, grad_weight)


def solution(mesh):
    placed = (P("tp", "ctx"),) * 5 + (P("tp", None),)
    return jax.shard_map(
        shards,
        mesh=mesh,
        in_specs=placed,
        out_specs=(P("tp", "ctx"),) * 3 + (P("tp", None), P("ctx", "tp")),
        check_vma=False,
    )
```
